512 devices in a mesh: row: 8 (over x, core), col: 64 (over z, y).
Axes of the slice: x: 4, y: 4, z: 16, core: 2. Of those that a mesh axis runs over, the one named last changes fastest.
Arguments:
- impedance: bfloat16 [2, 8192, 65536], P(None, 'col', 'row'), may hold values from -0.015625 to 0.015625
- tile_scale: float32 [512, 128], P('col', 'row'), may hold values from 0.5 to 2
- krylov_block: bfloat16 [65536, 128], P(('row', 'col')), may hold values from -6 to 6
- prior_basis: float32 [8192, 512], P(('col', 'row'))
Outputs:
- coefficients: float32 [256, 128], replicated
- new_basis: float32 [8192, 128], P(('col', 'row'))
The draws below stay inside these ranges and needn't reach their ends.
All inputs are finite; a program needn't handle non-finite values.
Results may differ from the reference program's by a relative error of at most 0.0003.
Values may be sent and summed in bfloat16 or wider, within the bound.
No kernel may reach another device: no remote copies, remote signals or barrier semaphores. Data moves between devices by JAX's collectives and lax.ppermute only.
A program may use at most 64 MiB of HBM per device.

```python
import math
import jax
import jax.numpy as jnp
from jax import lax

FIELDS = 64
PRIOR_BLOCKS = 4
TILE_ROWS = 16
TILE_COLS = 512
ROWS = 8192
ORDER = 65536


def draw_prior_basis(key, part):
    key = jax.random.fold_in(key, 7)
    subkeys = jax.random.split(key, 4)
    mixing = 0.5
    column_top = 3.0
    independent = jnp.clip(jax.random.normal(subkeys[0], (ROWS, PRIOR_BLOCKS, 2, FIELDS), jnp.float32), -6.0, 6.0)
    shared = jnp.clip(jax.random.normal(subkeys[1], (ROWS, 1, 2, FIELDS), jnp.float32), -6.0, 6.0)
    column_scale = jnp.exp(jax.random.uniform(subkeys[2], (1, PRIOR_BLOCKS, 1, FIELDS), jnp.float32, 0.0, math.log(column_top)))
    row_scale = jnp.exp(jax.random.uniform(subkeys[3], (ROWS, 1, 1, 1), jnp.float32, 0.0, math.log(8.0)))
    row_spread = math.sqrt(63.0 / (2.0 * math.log(8.0)))
    mixed = math.sqrt(1.0 - mixing) * independent + math.sqrt(mixing) * shared
    entries = mixed * column_scale * row_scale / (row_spread * math.sqrt(2.0 * ROWS))
    return entries.reshape(ROWS, PRIOR_BLOCKS * 2 * FIELDS).astype(jnp.float32)


def level_of(rng, shape, cuts, low, high):
    loudness, own = 1.0, jax.random.fold_in(rng, 6)
    for position, parts in cuts:
        steps = jnp.exp(jax.random.uniform(jax.random.fold_in(own, position), (parts,), jnp.float32, low / len(cuts), high / len(cuts)))
        loudness = loudness * jnp.repeat(steps, shape[position] // parts).reshape([-1 if axis == position else 1 for axis in range(len(shape))])
    return loudness


def bell_draw(rng, dims, spread, bound, cuts=(), held_as=jnp.bfloat16):
    loudness = level_of(rng, dims, cuts, -0.22, 0.18) if cuts else 1.0
    result = jax.random.normal(rng, dims, jnp.float32) * spread * loudness
    return jnp.minimum(jnp.maximum(result, -bound), bound).astype(held_as)


def setup_inputs(seed: int = 0) -> dict:
    keys = jax.random.split(jax.random.key(seed), 5)
    impedance = bell_draw(keys[0], (2, ROWS, ORDER), (2 * ORDER) ** -0.5, 0.015625, ((1, 64), (2, 8)))
    tile_scale = jnp.clip(jnp.exp(math.log(2.0) - 1.3862944 * jax.random.uniform(keys[1], (ROWS // TILE_ROWS, ORDER // TILE_COLS), jnp.float32) ** level_of(keys[1], (ROWS // TILE_ROWS, ORDER // TILE_COLS), ((0, 64), (1, 8)), -0.2, 0.2)), 0.5, 2.0)
    krylov_block = bell_draw(keys[2], (ORDER, 2 * FIELDS), 1.0, 6.0, ((0, 512),))
    prior_basis = draw_prior_basis(jax.random.fold_in(keys[4], 71), 0)
    return {"impedance": impedance, "tile_scale": tile_scale, "krylov_block": krylov_block, "prior_basis": prior_basis}


def split_blocks(matrix, blocks):
    row_count = matrix.shape[0]
    columns = matrix.shape[1] // (2 * blocks)
    shaped = matrix.reshape(row_count, blocks, 2, columns)
    return (shaped[:, :, 0, :].reshape(row_count, blocks * columns), shaped[:, :, 1, :].reshape(row_count, blocks * columns))

def inner_sum(left, right):
    return jnp.einsum('ra,rb->ab', left, right, precision=lax.Precision.HIGHEST)

def apply_basis(matrix, vector):
    return jnp.dot(matrix, vector, precision=lax.Precision.HIGHEST)

def combine_complex(running, angles):
    real_part = running[0][:, :angles] - running[1][:, angles:]
    imag_part = running[0][:, angles:] + running[1][:, :angles]
    return (real_part, imag_part)

def reference(impedance, tile_scale, krylov_block, prior_basis):
    tiles = ORDER // TILE_COLS

    def add_tile(running, tile_index):
        start = tile_index * TILE_COLS
        columns = lax.dynamic_slice_in_dim(impedance, start, TILE_COLS, 2).astype(jnp.float32)
        entries = lax.dynamic_slice_in_dim(krylov_block, start, TILE_COLS, 0).astype(jnp.float32)
        product = jnp.einsum('arc,cb->arb', columns, entries, precision=lax.Precision.HIGHEST)
        scales = jnp.repeat(lax.dynamic_slice_in_dim(tile_scale, tile_index, 1, 1)[:, 0], TILE_ROWS)
        return (running + product * scales[None, :, None], None)
    running, unused = lax.scan(add_tile, jnp.zeros((2, ROWS, 2 * FIELDS), jnp.float32), jnp.arange(tiles, dtype=jnp.int32))
    y_real, y_imag = combine_complex(running, FIELDS)
    basis_real, basis_imag = split_blocks(prior_basis, PRIOR_BLOCKS)
    coeff_real = inner_sum(basis_real, y_real) + inner_sum(basis_imag, y_imag)
    coeff_imag = inner_sum(basis_real, y_imag) - inner_sum(basis_imag, y_real)
    resid_real = y_real - (apply_basis(basis_real, coeff_real) - apply_basis(basis_imag, coeff_imag))
    resid_imag = y_imag - (apply_basis(basis_real, coeff_imag) + apply_basis(basis_imag, coeff_real))
    squares = lax.optimization_barrier(jnp.sum(resid_real * resid_real + resid_imag * resid_imag, axis=0))
    factor = 1.0 / jnp.sqrt(squares / ROWS + 1e-06)
    coefficients = jnp.concatenate([coeff_real, coeff_imag], 1)
    new_basis = jnp.concatenate([resid_real * factor[None, :], resid_imag * factor[None, :]], 1)
    return (coefficients, new_basis)
```

```python
import jax
import jax.numpy as jnp
from jax import lax
from jax.sharding import Mesh, PartitionSpec as P

ROW = ("x", "core")
COL = ("z", "y")
PLANE = ("x", "core", "y")
HIGHEST = lax.Precision.HIGHEST


def spread(block, axes):
    size = lax.axis_size(axes)
    copies = jnp.broadcast_to(block[None], (size,) + block.shape)
    return lax.all_to_all(copies, axes, 0, 0, tiled=True)


def scatter_sum(block, axes):
    size = lax.axis_size(axes)
    parts = block.reshape((size, block.shape[0] // size) + block.shape[1:])
    return jnp.sum(lax.all_to_all(parts, axes, 0, 0, tiled=True), axis=0)


def slab_product(impedance, tile_scale, entries):
    ys, zs, depth, columns = entries.shape
    rows = impedance.shape[1]
    tile_height = rows // tile_scale.shape[0]
    pieces = impedance.reshape(2, rows, zs, ys, depth)
    products = jnp.einsum("arzyi,yzib->zarb", pieces, entries, preferred_element_type=jnp.float32)
    scales = jnp.repeat(tile_scale, tile_height, axis=0).T
    running = jnp.sum(products * scales[:, None, :, None], axis=0)
    half = columns // 2
    real = running[0][:, :half] - running[1][:, half:]
    imag = running[0][:, half:] + running[1][:, :half]
    return jnp.concatenate([real, imag], 1)


def project(basis, product, blocks):
    half = product.shape[1] // 2
    inner = jnp.einsum("ra,rb->ab", basis, product, precision=HIGHEST)
    inner = inner.reshape(blocks, 2, half, 2 * half)
    from_real, from_imag = inner[:, 0], inner[:, 1]
    real = from_real[..., :half] + from_imag[..., half:]
    imag = from_real[..., half:] - from_imag[..., :half]
    return jnp.concatenate([real, imag], -1).reshape(blocks * half, 2 * half)


def subtract(basis, product, coefficients, blocks):
    half = product.shape[1] // 2
    shaped = coefficients.reshape(blocks, half, 2 * half)
    turned = jnp.concatenate([-shaped[..., half:], shaped[..., :half]], -1)
    both = jnp.stack([shaped, turned], 1).reshape(2 * blocks * half, 2 * half)
    return product - jnp.dot(basis, both, precision=HIGHEST)


def per_device(impedance, tile_scale, krylov_block, prior_basis):
    columns = krylov_block.shape[1]
    half = columns // 2
    blocks = prior_basis.shape[1] // columns
    with jax.named_scope("entries_z"):
        along_z = spread(krylov_block, "z")
    with jax.named_scope("entries_y"):
        entries = spread(along_z, "y")
    with jax.named_scope("slab"):
        partial = slab_product(impedance, tile_scale, entries)
    with jax.named_scope("product_rows"):
        product = scatter_sum(partial, ROW)
    with jax.named_scope("project"):
        local = project(prior_basis, product, blocks)
    with jax.named_scope("coefficients_plane"):
        chunk = scatter_sum(local, PLANE)
    with jax.named_scope("coefficients_z"):
        chunk = jnp.sum(spread(chunk, "z"), axis=0)
    with jax.named_scope("coefficients_all"):
        coefficients = spread(chunk, PLANE).reshape(blocks * half, columns)
    with jax.named_scope("residual"):
        residual = subtract(prior_basis, product, coefficients, blocks)
    with jax.named_scope("squares"):
        sums = jnp.sum(residual * residual, axis=0)
        sums = jnp.sum(spread(sums, ("x", "y")), axis=0)
        sums = jnp.sum(spread(sums, ("core", "z")), axis=0)
        squares = sums[:half] + sums[half:]
    with jax.named_scope("scale"):
        total_rows = prior_basis.shape[0] * lax.axis_size(ROW + COL)
        factor = 1.0 / jnp.sqrt(squares / total_rows + 1e-06)
        new_basis = residual * jnp.concatenate([factor, factor])[None, :]
    return (coefficients, new_basis)


def solution(mesh):
    rows = 4 if mesh.shape["row"] % 4 == 0 else 1
    devices = mesh.devices.reshape(rows, mesh.shape["row"] // rows, mesh.shape["col"] // 4, 4)
    fine = Mesh(devices, ("x", "core", "z", "y"))
    return jax.shard_map(
        per_device,
        mesh=fine,
        in_specs=(
            P(None, COL, ROW),
            P(COL, ROW),
            P(ROW + COL, None),
            P(COL + ROW, None),
        ),
        out_specs=(P(), P(COL + ROW, None)),
        check_vma=False,
    )
```

```python
import functools

import jax
import jax.numpy as jnp
from jax import lax
from jax.experimental import pallas as pl
from jax.experimental.pallas import tpu as pltpu
from jax.sharding import Mesh, PartitionSpec as P

ROW = ("x", "core")
COL = ("z", "y")
PLANE = ("x", "core", "y")
HIGHEST = lax.Precision.HIGHEST


def spread(block, axes):
    size = lax.axis_size(axes)
    copies = jnp.broadcast_to(block[None], (size,) + block.shape)
    return lax.all_to_all(copies, axes, 0, 0, tiled=True)


def ring_gather(block, axis):
    size = lax.axis_size(axis)
    me = lax.axis_index(axis)
    stacked = jnp.zeros((size,) + block.shape, block.dtype)
    for step in range(size):
        pairs = [(member, (member + step) % size) for member in range(size)]
        arrived = lax.ppermute(block, axis, pairs) if step else block
        owner = lax.rem(me - step + size, size)
        stacked = lax.dynamic_update_index_in_dim(stacked, arrived, owner, 0)
    return stacked


def turn(block, first, second):
    half = block.shape[1] // 2
    lanes = lax.broadcasted_iota(jnp.int32, block.shape, 1)
    return pltpu.roll(block, half, 1) * jnp.where(lanes < half, first, second)


def slab_kernel(chunks, impedance, scales, entries, basis, out, held, sems):
    rows, columns = scales.shape[0], entries.shape[3]
    ys, zs, depth, _ = entries.shape
    width = ys * depth
    members, height, _ = out.shape
    share = rows // members
    span = zs * width // chunks
    copies = []
    for chunk in range(chunks):
        part = pl.ds(chunk * span, span)
        copies.append(pltpu.make_async_copy(impedance.at[:, :, part], held.at[:, :, part], sems.at[chunk]))
        copies[-1].start()
    running = jnp.zeros((2, rows, columns), jnp.float32)
    for tile in range(zs):
        if tile % (zs // chunks) == 0:
            copies[tile // (zs // chunks)].wait()
        piece = held[:, :, tile * width : (tile + 1) * width].reshape(2 * rows, width)
        block = entries[:, tile].reshape(width, columns)
        product = jnp.dot(piece, block, preferred_element_type=jnp.float32)
        running += product.reshape(2, rows, columns) * scales[:, tile : tile + 1][None]
    partial = running[0] + turn(running[1], -1.0, 1.0)
    inner = jnp.dot(basis[...], partial, precision=HIGHEST, preferred_element_type=jnp.float32)
    half = columns // 2
    inner = inner.reshape(-1, 2, half, columns)
    sums = inner[:, 0].reshape(-1, columns) + turn(inner[:, 1].reshape(-1, columns), 1.0, -1.0)
    out[:, : height - share, :] = sums.reshape(members, height - share, columns)
    for member in range(members):
        out[member, height - share :, :] = partial[member * share : (member + 1) * share]


def slab_sums(impedance, scales, entries, basis, members):
    rows = impedance.shape[1]
    columns = entries.shape[3]
    chunks = 4
    height = (basis.shape[0] // 2 + rows) // members
    vmem = pl.BlockSpec(memory_space=pltpu.VMEM)
    return pl.pallas_call(
        functools.partial(slab_kernel, chunks),
        out_shape=jax.ShapeDtypeStruct((members, height, columns), jnp.float32),
        in_specs=[pl.BlockSpec(memory_space=pltpu.HBM), vmem, vmem, vmem],
        out_specs=vmem,
        scratch_shapes=[pltpu.VMEM(impedance.shape, impedance.dtype), pltpu.SemaphoreType.DMA((chunks,))],
        compiler_params=pltpu.CompilerParams(vmem_limit_bytes=48 * 2**20),
        cost_estimate=pl.CostEstimate(
            flops=4 * impedance.shape[2] * rows * columns,
            bytes_accessed=2 * (impedance.size + entries.size),
            transcendentals=0,
        ),
    )(impedance, scales, entries, basis)


def residual_kernel(taken, basis, coefficients, residual, sums):
    members, height, columns = taken.shape
    count = coefficients.shape[0]
    half = columns // 2
    found = taken[:, : count // members, :].reshape(count, columns)
    product = taken[:, count // members :, :].reshape(residual.shape)
    coefficients[...] = found
    turned = turn(found, -1.0, 1.0)
    pair = [found.reshape(-1, 1, half, columns), turned.reshape(-1, 1, half, columns)]
    both = jnp.concatenate(pair, 1).reshape(2 * count, columns)
    rest = product - jnp.dot(basis[...], both, precision=HIGHEST, preferred_element_type=jnp.float32)
    residual[...] = rest
    sums[...] = jnp.broadcast_to(jnp.sum(rest * rest, axis=0, keepdims=True), sums.shape)


def plane_residual(taken, basis, copies):
    members, height, columns = taken.shape
    rows, width = basis.shape
    vmem = pl.BlockSpec(memory_space=pltpu.VMEM)
    shapes = [(width // 2, columns), (rows, columns), (copies, columns)]
    return pl.pallas_call(
        residual_kernel,
        out_shape=[jax.ShapeDtypeStruct(shape, jnp.float32) for shape in shapes],
        in_specs=[vmem, vmem],
        out_specs=[vmem] * 3,
        compiler_params=pltpu.CompilerParams(vmem_limit_bytes=24 * 2**20),
        cost_estimate=pl.CostEstimate(
            flops=12 * rows * width * columns,
            bytes_accessed=4 * (taken.size + basis.size + rows * columns),
            transcendentals=0,
        ),
    )(taken, basis)


def per_device(impedance, tile_scale, krylov_block, prior_basis):
    columns = krylov_block.shape[1]
    half = columns // 2
    width = prior_basis.shape[1]
    own_rows = prior_basis.shape[0]
    rows = impedance.shape[1]
    ys, zs, row_members, members = (lax.axis_size(axes) for axes in ("y", "z", ROW, PLANE))
    share = rows // members
    height = width // 2 // members
    with jax.named_scope("basis_pair"):
        pair = ring_gather(ring_gather(prior_basis, "y"), "core")
    with jax.named_scope("entries_z"):
        along_z = spread(krylov_block, "z")
    with jax.named_scope("entries_y"):
        along_z, pair = lax.optimization_barrier((along_z, pair))
        entries = spread(along_z, "y")
    with jax.named_scope("basis_plane"):
        gathered = ring_gather(pair, "x").reshape(row_members, ys, own_rows, width)
        here = lax.dynamic_index_in_dim(gathered, lax.axis_index("y"), 1, False).reshape(rows, width).T
        basis = gathered.reshape(row_members, ys, own_rows // share, share, width)
        basis = jnp.swapaxes(basis, 1, 2).reshape(members * ys * share, width)
        row, y = lax.axis_index(ROW).astype(jnp.int32), lax.axis_index("y").astype(jnp.int32)
        scales = jnp.repeat(tile_scale, rows // tile_scale.shape[0], axis=0)
        entries, here, basis, scales, row, y = lax.optimization_barrier((entries, here, basis, scales, row, y))
    with jax.named_scope("slab"):
        parts = slab_sums(impedance, scales, entries, here, members)
    with jax.named_scope("sums_plane"):
        taken = lax.all_to_all(parts, PLANE, 0, 0, tiled=True)
        chunk = jnp.sum(taken[:, :height], axis=0)
        product = jnp.sum(taken[:, height:].reshape(row_members, ys * share, columns), axis=0)
        chunk, product = lax.optimization_barrier((chunk, product))
    with jax.named_scope("coefficients_z"):
        chunk = jnp.sum(spread(chunk, "z"), axis=0)
    with jax.named_scope("gather_plane"):
        taken = spread(jnp.concatenate([chunk, product], 0), PLANE)
    with jax.named_scope("residual"):
        coefficients, residual, sums = plane_residual(taken, basis, zs)
        own = residual.reshape(row_members, own_rows // share, ys, share, columns)
        sizes = (1, own_rows // share, 1, share, columns)
        zero = jnp.int32(0)
        own = lax.dynamic_slice(own, (row, zero, y, zero, zero), sizes, allow_negative_indices=False)
        own = own.reshape(own_rows, columns)
        own, sums = lax.optimization_barrier((own, sums))
    with jax.named_scope("squares"):
        sums = jnp.sum(lax.all_to_all(sums, "z", 0, 0, tiled=True), axis=0)
        squares = sums[:half] + sums[half:]
    with jax.named_scope("scale"):
        total_rows = own_rows * lax.axis_size(ROW + COL)
        factor = 1.0 / jnp.sqrt(squares / total_rows + 1e-06)
        new_basis = own * jnp.concatenate([factor, factor])[None, :]
    return (coefficients, new_basis)


def solution(mesh):
    rows = 4 if mesh.shape["row"] % 4 == 0 else 1
    devices = mesh.devices.reshape(rows, mesh.shape["row"] // rows, mesh.shape["col"] // 4, 4)
    fine = Mesh(devices, ("x", "core", "z", "y"))
    return jax.shard_map(
        per_device,
        mesh=fine,
        in_specs=(
            P(None, COL, ROW),
            P(COL, ROW),
            P(ROW + COL, None),
            P(COL + ROW, None),
        ),
        out_specs=(P(), P(COL + ROW, None)),
        check_vma=False,
    )
```

```python
import functools

import jax
import jax.numpy as jnp
from jax import lax
from jax.experimental import pallas as pl
from jax.experimental.pallas import tpu as pltpu
from jax.experimental.layout import Layout, with_layout_constraint
from jax.sharding import Mesh, PartitionSpec as P

ROW = ("x", "core")
COL = ("z", "y")
PLANE = ("x", "core", "y")
HIGHEST = lax.Precision.HIGHEST


def spread(block, axes):
    size = lax.axis_size(axes)
    copies = jnp.broadcast_to(block[None], (size,) + block.shape)
    return lax.all_to_all(copies, axes, 0, 0, tiled=True)


def ring_gather(block, axis):
    size = lax.axis_size(axis)
    me = lax.axis_index(axis)
    stacked = jnp.zeros((size,) + block.shape, block.dtype)
    for step in range(size):
        pairs = [(member, (member + step) % size) for member in range(size)]
        arrived = lax.ppermute(block, axis, pairs) if step else block
        owner = lax.rem(me - step + size, size)
        stacked = lax.dynamic_update_index_in_dim(stacked, arrived, owner, 0)
    return stacked


def turn(block, first, second):
    half = block.shape[1] // 2
    lanes = lax.broadcasted_iota(jnp.int32, block.shape, 1)
    return pltpu.roll(block, half, 1) * jnp.where(lanes < half, first, second)


def slab_kernel(chunks, impedance, scales, entries, basis, out, held, sems):
    rows, columns = scales.shape[0], entries.shape[3]
    ys, zs, depth, _ = entries.shape
    width = ys * depth
    members, height, _ = out.shape
    share = rows // members
    span = zs * width // chunks
    copies = []
    for chunk in range(chunks):
        part = pl.ds(chunk * span, span)
        copies.append(pltpu.make_async_copy(impedance.at[:, :, part], held.at[:, :, part], sems.at[chunk]))
        copies[-1].start()
    running = jnp.zeros((2, rows, columns), jnp.float32)
    for tile in range(zs):
        if tile % (zs // chunks) == 0:
            copies[tile // (zs // chunks)].wait()
        piece = held[:, :, tile * width : (tile + 1) * width].reshape(2 * rows, width)
        block = entries[:, tile].reshape(width, columns)
        product = jnp.dot(piece, block, preferred_element_type=jnp.float32)
        running += product.reshape(2, rows, columns) * scales[:, tile : tile + 1][None]
    partial = running[0] + turn(running[1], -1.0, 1.0)
    inner = jnp.dot(basis[...], partial, precision=HIGHEST, preferred_element_type=jnp.float32)
    half = columns // 2
    inner = inner.reshape(-1, 2, half, columns)
    sums = inner[:, 0].reshape(-1, columns) + turn(inner[:, 1].reshape(-1, columns), 1.0, -1.0)
    out[:, : height - share, :] = sums.reshape(members, height - share, columns)
    for member in range(members):
        out[member, height - share :, :] = partial[member * share : (member + 1) * share]


def slab_sums(impedance, scales, entries, basis, members):
    rows = impedance.shape[1]
    columns = entries.shape[3]
    chunks = 4
    height = (basis.shape[0] // 2 + rows) // members
    vmem = pl.BlockSpec(memory_space=pltpu.VMEM)
    return pl.pallas_call(
        functools.partial(slab_kernel, chunks),
        out_shape=jax.ShapeDtypeStruct((members, height, columns), jnp.float32),
        in_specs=[pl.BlockSpec(memory_space=pltpu.HBM), vmem, vmem, vmem],
        out_specs=vmem,
        scratch_shapes=[pltpu.VMEM(impedance.shape, impedance.dtype), pltpu.SemaphoreType.DMA((chunks,))],
        compiler_params=pltpu.CompilerParams(vmem_limit_bytes=48 * 2**20),
        cost_estimate=pl.CostEstimate(
            flops=4 * impedance.shape[2] * rows * columns,
            bytes_accessed=2 * (impedance.size + entries.size),
            transcendentals=0,
        ),
    )(impedance, scales, entries, basis)


def residual_kernel(taken, basis, coefficients, residual, sums, product):
    members, height, columns = taken.shape
    rows, width = basis.shape
    count = coefficients.shape[0]
    half = columns // 2
    head = count // members
    share = rows // members
    for member in range(members):
        product[member * share : (member + 1) * share] = taken[member, head:]
    found = taken[:, :head, :].reshape(count, columns)
    coefficients[...] = found
    turned = turn(found, -1.0, 1.0)
    pair = [found.reshape(-1, 1, half, columns), turned.reshape(-1, 1, half, columns)]
    both = jnp.concatenate(pair, 1).reshape(width, columns)
    known = jnp.dot(basis[...], both, precision=HIGHEST, preferred_element_type=jnp.float32)
    rest = product[...] - known
    residual[...] = rest
    sums[...] = jnp.broadcast_to(jnp.sum(rest * rest, axis=0, keepdims=True), sums.shape)


def rows_residual(taken, basis, copies):
    columns = taken.shape[2]
    rows, width = basis.shape
    vmem = pl.BlockSpec(memory_space=pltpu.VMEM)
    shapes = [(width // 2, columns), (rows, columns), (copies, columns)]
    return pl.pallas_call(
        residual_kernel,
        out_shape=[jax.ShapeDtypeStruct(shape, jnp.float32) for shape in shapes],
        in_specs=[vmem, vmem],
        out_specs=[vmem] * 3,
        scratch_shapes=[pltpu.VMEM((rows, columns), jnp.float32)],
        compiler_params=pltpu.CompilerParams(vmem_limit_bytes=24 * 2**20),
        cost_estimate=pl.CostEstimate(
            flops=12 * rows * width * columns,
            bytes_accessed=4 * (taken.size + basis.size + rows * columns),
            transcendentals=0,
        ),
    )(taken, basis)


def per_device(impedance, tile_scale, krylov_block, prior_basis):
    columns = krylov_block.shape[1]
    half = columns // 2
    width = prior_basis.shape[1]
    own_rows = prior_basis.shape[0]
    rows = impedance.shape[1]
    ys, row_members, members = (lax.axis_size(axes) for axes in ("y", ROW, PLANE))
    share = rows // members
    height = width // 2 // members
    with jax.named_scope("entries_z"):
        along_z = lax.all_gather(krylov_block, "z", axis=0)
        along_z, prior = lax.optimization_barrier((along_z, prior_basis))
    with jax.named_scope("entries_y"):
        entries = spread(along_z, "y")
    with jax.named_scope("basis_rows"):
        here = ring_gather(ring_gather(prior, "core"), "x").reshape(rows, width)
    with jax.named_scope("stage"):
        scales = jnp.repeat(tile_scale, rows // tile_scale.shape[0], axis=0)
        start = (lax.axis_index(ROW) * own_rows).astype(jnp.int32)
        turned = with_layout_constraint(here.T, Layout((0, 1)))
        held = (entries, scales, here, turned, start)
        entries, scales, here, turned, start = lax.optimization_barrier(held)
    with jax.named_scope("slab"):
        parts = slab_sums(impedance, scales, entries, turned, members)
    with jax.named_scope("sums_plane"):
        taken = lax.all_to_all(parts, PLANE, 0, 0, tiled=True)
        chunk = jnp.sum(taken[:, :height], axis=0)
        product = jnp.sum(taken[:, height:].reshape(row_members, ys, share, columns), axis=0)
        chunk, product = lax.optimization_barrier((chunk, product))
    with jax.named_scope("coefficients_z"):
        chunk = jnp.sum(spread(chunk, "z"), axis=0)
    with jax.named_scope("gather_plane"):
        parts = jnp.broadcast_to(product[None], (row_members,) + product.shape).reshape(members, share, columns)
        parts = jnp.concatenate([jnp.broadcast_to(chunk[None], (members,) + chunk.shape), parts], 1)
        taken = lax.all_to_all(parts, PLANE, 0, 0, tiled=True)
    with jax.named_scope("residual"):
        coefficients, residual, sums = rows_residual(taken, here, lax.axis_size(COL))
        zero = jnp.int32(0)
        own = lax.dynamic_slice(residual, (start, zero), (own_rows, columns), allow_negative_indices=False)
        own, sums = lax.optimization_barrier((own, sums))
    with jax.named_scope("squares"):
        sums = jnp.sum(lax.all_to_all(sums, COL, 0, 0, tiled=True), axis=0)
        squares = sums[:half] + sums[half:]
    with jax.named_scope("scale"):
        total_rows = own_rows * lax.axis_size(ROW + COL)
        factor = 1.0 / jnp.sqrt(squares / total_rows + 1e-06)
        new_basis = own * jnp.concatenate([factor, factor])[None, :]
    return (coefficients, new_basis)


def solution(mesh):
    rows = 4 if mesh.shape["row"] % 4 == 0 else 1
    devices = mesh.devices.reshape(rows, mesh.shape["row"] // rows, mesh.shape["col"] // 4, 4)
    fine = Mesh(devices, ("x", "core", "z", "y"))
    return jax.shard_map(
        per_device,
        mesh=fine,
        in_specs=(
            P(None, COL, ROW),
            P(COL, ROW),
            P(ROW + COL, None),
            P(COL + ROW, None),
        ),
        out_specs=(P(), P(COL + ROW, None)),
        check_vma=False,
    )
```

```python
import functools

import jax
import jax.numpy as jnp
from jax import lax
from jax.experimental import pallas as pl
from jax.experimental.pallas import tpu as pltpu
from jax.experimental.layout import Layout, with_layout_constraint
from jax.sharding import Mesh, PartitionSpec as P

ROW = ("x", "core")
COL = ("z", "y")
PLANE = ("x", "core", "y")
HIGHEST = lax.Precision.HIGHEST


def spread(block, axes):
    size = lax.axis_size(axes)
    copies = jnp.broadcast_to(block[None], (size,) + block.shape)
    return lax.all_to_all(copies, axes, 0, 0, tiled=True)


def ring_gather(block, axis):
    size = lax.axis_size(axis)
    me = lax.axis_index(axis)
    stacked = jnp.zeros((size,) + block.shape, block.dtype)
    for step in range(size):
        pairs = [(member, (member + step) % size) for member in range(size)]
        arrived = lax.ppermute(block, axis, pairs) if step else block
        owner = lax.rem(me - step + size, size)
        stacked = lax.dynamic_update_index_in_dim(stacked, arrived, owner, 0)
    return stacked


def turn(block, first, second):
    half = block.shape[1] // 2
    lanes = lax.broadcasted_iota(jnp.int32, block.shape, 1)
    return pltpu.roll(block, half, 1) * jnp.where(lanes < half, first, second)


def copies_kernel(source, out, sems):
    size = out.shape[0]
    copies = [pltpu.make_async_copy(source, out.at[i], sems.at[i]) for i in range(size)]
    for copy in copies:
        copy.start()
    for copy in copies:
        copy.wait()


def copies_of(block, size):
    return pl.pallas_call(
        copies_kernel,
        out_shape=jax.ShapeDtypeStruct((size,) + block.shape, block.dtype),
        in_specs=[pl.BlockSpec(memory_space=pltpu.VMEM)],
        out_specs=pl.BlockSpec(memory_space=pltpu.HBM),
        scratch_shapes=[pltpu.SemaphoreType.DMA((size,))],
        compiler_params=pltpu.CompilerParams(vmem_limit_bytes=8 * 2**20),
    )(block)


def slab_kernel(chunks, impedance, scales, entries, basis, out, held, sems):
    rows, columns = scales.shape[0], entries.shape[3]
    ys, zs, depth, _ = entries.shape
    width = ys * depth
    members, height, _ = out.shape
    share = rows // members
    span = zs * width // chunks
    copies = []
    for chunk in range(chunks):
        part = pl.ds(chunk * span, span)
        copies.append(pltpu.make_async_copy(impedance.at[:, :, part], held.at[:, :, part], sems.at[chunk]))
        copies[-1].start()
    running = jnp.zeros((2, rows, columns), jnp.float32)
    for tile in range(zs):
        if tile % (zs // chunks) == 0:
            copies[tile // (zs // chunks)].wait()
        piece = held[:, :, tile * width : (tile + 1) * width].reshape(2 * rows, width)
        block = entries[:, tile].reshape(width, columns)
        product = jnp.dot(piece, block, preferred_element_type=jnp.float32)
        running += product.reshape(2, rows, columns) * scales[:, tile : tile + 1][None]
    partial = running[0] + turn(running[1], -1.0, 1.0)
    inner = jnp.dot(basis[...], partial, precision=HIGHEST, preferred_element_type=jnp.float32)
    half = columns // 2
    inner = inner.reshape(-1, 2, half, columns)
    sums = inner[:, 0].reshape(-1, columns) + turn(inner[:, 1].reshape(-1, columns), 1.0, -1.0)
    out[:, : height - share, :] = sums.reshape(members, height - share, columns)
    for member in range(members):
        out[member, height - share :, :] = partial[member * share : (member + 1) * share]


def slab_sums(impedance, scales, entries, basis, members):
    rows = impedance.shape[1]
    columns = entries.shape[3]
    chunks = 4
    height = (basis.shape[0] // 2 + rows) // members
    vmem = pl.BlockSpec(memory_space=pltpu.VMEM)
    return pl.pallas_call(
        functools.partial(slab_kernel, chunks),
        out_shape=jax.ShapeDtypeStruct((members, height, columns), jnp.float32),
        in_specs=[pl.BlockSpec(memory_space=pltpu.HBM), vmem, vmem, vmem],
        out_specs=vmem,
        scratch_shapes=[pltpu.VMEM(impedance.shape, impedance.dtype), pltpu.SemaphoreType.DMA((chunks,))],
        compiler_params=pltpu.CompilerParams(vmem_limit_bytes=48 * 2**20),
        cost_estimate=pl.CostEstimate(
            flops=4 * impedance.shape[2] * rows * columns,
            bytes_accessed=2 * (impedance.size + entries.size),
            transcendentals=0,
        ),
    )(impedance, scales, entries, basis)


def residual_kernel(taken, basis, residual, sums, product):
    members, height, columns = taken.shape
    rows, width = basis.shape
    count = width // 2
    half = columns // 2
    head = count // members
    share = rows // members
    for member in range(members):
        product[member * share : (member + 1) * share] = taken[member, head:]
    found = taken[:, :head, :].reshape(count, columns)
    turned = turn(found, -1.0, 1.0)
    pair = [found.reshape(-1, 1, half, columns), turned.reshape(-1, 1, half, columns)]
    both = jnp.concatenate(pair, 1).reshape(width, columns)
    known = jnp.dot(basis[...], both, precision=HIGHEST, preferred_element_type=jnp.float32)
    rest = product[...] - known
    residual[...] = rest
    sums[...] = jnp.broadcast_to(jnp.sum(rest * rest, axis=0, keepdims=True), sums.shape)


def rows_residual(taken, basis, copies):
    columns = taken.shape[2]
    rows, width = basis.shape
    vmem = pl.BlockSpec(memory_space=pltpu.VMEM)
    shapes = [(rows, columns), (copies, columns)]
    return pl.pallas_call(
        residual_kernel,
        out_shape=[jax.ShapeDtypeStruct(shape, jnp.float32) for shape in shapes],
        in_specs=[vmem, vmem],
        out_specs=[vmem] * 2,
        scratch_shapes=[pltpu.VMEM((rows, columns), jnp.float32)],
        compiler_params=pltpu.CompilerParams(vmem_limit_bytes=24 * 2**20),
        cost_estimate=pl.CostEstimate(
            flops=12 * rows * width * columns,
            bytes_accessed=4 * (taken.size + basis.size + rows * columns),
            transcendentals=0,
        ),
    )(taken, basis)


def scale_kernel(total_rows, sums, own, taken, coefficients, new_basis):
    count, columns = coefficients.shape
    coefficients[...] = taken[:, : count // taken.shape[0], :].reshape(count, columns)
    squares = sums[...] + turn(sums[...], 1.0, 1.0)
    factor = 1.0 / jnp.sqrt(squares / total_rows + 1e-06)
    new_basis[...] = own[...] * factor


def scaled(sums, own, taken, count, total_rows):
    columns = own.shape[1]
    vmem = pl.BlockSpec(memory_space=pltpu.VMEM)
    shapes = [(count, columns), own.shape]
    return pl.pallas_call(
        functools.partial(scale_kernel, total_rows),
        out_shape=[jax.ShapeDtypeStruct(shape, jnp.float32) for shape in shapes],
        in_specs=[vmem] * 3,
        out_specs=[vmem] * 2,
        compiler_params=pltpu.CompilerParams(vmem_limit_bytes=16 * 2**20),
    )(sums, own, taken)


def per_device(impedance, tile_scale, krylov_block, prior_basis):
    columns = krylov_block.shape[1]
    width = prior_basis.shape[1]
    own_rows = prior_basis.shape[0]
    rows = impedance.shape[1]
    ys, row_members, members = (lax.axis_size(axes) for axes in ("y", ROW, PLANE))
    share = rows // members
    height = width // 2 // members
    with jax.named_scope("entries_z"):
        along_z = lax.all_gather(krylov_block, "z", axis=0)
        along_z, prior = lax.optimization_barrier((along_z, prior_basis))
    with jax.named_scope("entries_y"):
        entries = lax.all_to_all(copies_of(along_z, ys), "y", 0, 0, tiled=True)
    with jax.named_scope("basis_rows"):
        here = ring_gather(ring_gather(prior, "core"), "x").reshape(rows, width)
    with jax.named_scope("stage"):
        scales = jnp.repeat(tile_scale, rows // tile_scale.shape[0], axis=0)
        start = (lax.axis_index(ROW) * own_rows).astype(jnp.int32)
        turned = with_layout_constraint(here.T, Layout((0, 1)))
        held = (entries, scales, here, turned, start)
        entries, scales, here, turned, start = lax.optimization_barrier(held)
    with jax.named_scope("slab"):
        parts = slab_sums(impedance, scales, entries, turned, members)
    with jax.named_scope("sums_plane"):
        taken = lax.all_to_all(parts, PLANE, 0, 0, tiled=True)
        chunk = jnp.sum(taken[:, :height], axis=0)
        product = jnp.sum(taken[:, height:].reshape(row_members, ys, share, columns), axis=0)
        chunk, product = lax.optimization_barrier((chunk, product))
    with jax.named_scope("coefficients_z"):
        chunk = jnp.sum(spread(chunk, "z"), axis=0)
    with jax.named_scope("gather_plane"):
        parts = jnp.broadcast_to(product[None], (row_members,) + product.shape).reshape(members, share, columns)
        parts = jnp.concatenate([jnp.broadcast_to(chunk[None], (members,) + chunk.shape), parts], 1)
        taken = lax.all_to_all(parts, PLANE, 0, 0, tiled=True)
    with jax.named_scope("residual"):
        residual, sums = rows_residual(taken, here, lax.axis_size(COL))
        zero = jnp.int32(0)
        own = lax.dynamic_slice(residual, (start, zero), (own_rows, columns), allow_negative_indices=False)
        own, sums = lax.optimization_barrier((own, sums))
    with jax.named_scope("squares"):
        sums = jnp.sum(lax.all_to_all(sums, COL, 0, 0, tiled=True), axis=0)
    with jax.named_scope("scale"):
        total_rows = own_rows * lax.axis_size(ROW + COL)
        coefficients, new_basis = scaled(sums[None], own, taken, width // 2, total_rows)
    return (coefficients, new_basis)


def solution(mesh):
    rows = 4 if mesh.shape["row"] % 4 == 0 else 1
    devices = mesh.devices.reshape(rows, mesh.shape["row"] // rows, mesh.shape["col"] // 4, 4)
    fine = Mesh(devices, ("x", "core", "z", "y"))
    return jax.shard_map(
        per_device,
        mesh=fine,
        in_specs=(
            P(None, COL, ROW),
            P(COL, ROW),
            P(ROW + COL, None),
            P(COL + ROW, None),
        ),
        out_specs=(P(), P(COL + ROW, None)),
        check_vma=False,
    )
```

```python
import functools

import jax
import jax.numpy as jnp
from jax import lax
from jax.experimental import pallas as pl
from jax.experimental.pallas import tpu as pltpu
from jax.experimental.layout import Layout, with_layout_constraint
from jax.sharding import Mesh, PartitionSpec as P

ROW = ("x", "core")
COL = ("z", "y")
PLANE = ("x", "core", "y")
HIGHEST = lax.Precision.HIGHEST


def spread(block, axes):
    size = lax.axis_size(axes)
    copies = jnp.broadcast_to(block[None], (size,) + block.shape)
    return lax.all_to_all(copies, axes, 0, 0, tiled=True)


def ring_gather(block, axis):
    size = lax.axis_size(axis)
    me = lax.axis_index(axis)
    stacked = jnp.zeros((size,) + block.shape, block.dtype)
    for step in range(size):
        pairs = [(member, (member + step) % size) for member in range(size)]
        arrived = lax.ppermute(block, axis, pairs) if step else block
        owner = lax.rem(me - step + size, size)
        stacked = lax.dynamic_update_index_in_dim(stacked, arrived, owner, 0)
    return stacked


def turn(block, first, second):
    half = block.shape[1] // 2
    lanes = lax.broadcasted_iota(jnp.int32, block.shape, 1)
    return pltpu.roll(block, half, 1) * jnp.where(lanes < half, first, second)


def copies_kernel(source, out, sems):
    size = out.shape[0]
    copies = [pltpu.make_async_copy(source, out.at[i], sems.at[i]) for i in range(size)]
    for copy in copies:
        copy.start()
    for copy in copies:
        copy.wait()


def copies_of(block, size):
    return pl.pallas_call(
        copies_kernel,
        out_shape=jax.ShapeDtypeStruct((size,) + block.shape, block.dtype),
        in_specs=[pl.BlockSpec(memory_space=pltpu.VMEM)],
        out_specs=pl.BlockSpec(memory_space=pltpu.HBM),
        scratch_shapes=[pltpu.SemaphoreType.DMA((size,))],
        compiler_params=pltpu.CompilerParams(vmem_limit_bytes=8 * 2**20),
    )(block)


def slab_kernel(chunks, impedance, scales, entries, basis, out, held, sems):
    rows, columns = scales.shape[0], entries.shape[3]
    ys, zs, depth, _ = entries.shape
    width = ys * depth
    members, share, _ = out.shape
    span = zs * width // chunks
    copies = []
    for chunk in range(chunks):
        part = pl.ds(chunk * span, span)
        copies.append(pltpu.make_async_copy(impedance.at[:, :, part], held.at[:, :, part], sems.at[chunk]))
        copies[-1].start()
    running = jnp.zeros((2, rows, columns), jnp.float32)
    for tile in range(zs):
        if tile % (zs // chunks) == 0:
            copies[tile // (zs // chunks)].wait()
        piece = held[:, :, tile * width : (tile + 1) * width].reshape(2 * rows, width)
        block = entries[:, tile].reshape(width, columns)
        product = jnp.dot(piece, block, preferred_element_type=jnp.float32)
        running += product.reshape(2, rows, columns) * scales[:, tile : tile + 1][None]
    partial = running[0] + turn(running[1], -1.0, 1.0)
    inner = jnp.dot(basis[...], partial, precision=HIGHEST, preferred_element_type=jnp.float32)
    half = columns // 2
    inner = inner.reshape(-1, 2, half, columns)
    sums = inner[:, 0].reshape(-1, columns) + turn(inner[:, 1].reshape(-1, columns), 1.0, -1.0)
    step = sums.shape[0] // members
    for member in range(members):
        for first in range(0, step, share):
            lanes = slice(first // share * columns, (first // share + 1) * columns)
            out[member, :, lanes] = sums[member * step + first : member * step + first + share]
        out[member, :, step // share * columns :] = partial[member * share : (member + 1) * share]


def slab_sums(impedance, scales, entries, basis, members):
    rows = impedance.shape[1]
    columns = entries.shape[3]
    chunks = 4
    share = rows // members
    lanes = (basis.shape[0] // 2 // rows + 1) * columns
    vmem = pl.BlockSpec(memory_space=pltpu.VMEM)
    return pl.pallas_call(
        functools.partial(slab_kernel, chunks),
        out_shape=jax.ShapeDtypeStruct((members, share, lanes), jnp.float32),
        in_specs=[pl.BlockSpec(memory_space=pltpu.HBM), vmem, vmem, vmem],
        out_specs=vmem,
        scratch_shapes=[pltpu.VMEM(impedance.shape, impedance.dtype), pltpu.SemaphoreType.DMA((chunks,))],
        compiler_params=pltpu.CompilerParams(vmem_limit_bytes=48 * 2**20),
        cost_estimate=pl.CostEstimate(
            flops=4 * impedance.shape[2] * rows * columns,
            bytes_accessed=2 * (impedance.size + entries.size),
            transcendentals=0,
        ),
    )(impedance, scales, entries, basis)


def unpack(taken, found):
    members, share, _ = taken.shape
    columns = found.shape[1]
    step = found.shape[0] // members
    for member in range(members):
        for first in range(0, step, share):
            lanes = slice(first // share * columns, (first // share + 1) * columns)
            found[member * step + first : member * step + first + share] = taken[member, :, lanes]


def residual_kernel(taken, basis, residual, sums, product, found):
    members, share, _ = taken.shape
    rows, width = basis.shape
    count, columns = found.shape
    half = columns // 2
    for member in range(members):
        product[member * share : (member + 1) * share] = taken[member, :, count // rows * columns :]
    unpack(taken, found)
    turned = turn(found[...], -1.0, 1.0)
    pair = [found[...].reshape(-1, 1, half, columns), turned.reshape(-1, 1, half, columns)]
    both = jnp.concatenate(pair, 1).reshape(width, columns)
    known = jnp.dot(basis[...], both, precision=HIGHEST, preferred_element_type=jnp.float32)
    rest = product[...] - known
    residual[...] = rest
    sums[...] = jnp.broadcast_to(jnp.sum(rest * rest, axis=0, keepdims=True), sums.shape)


def rows_residual(taken, basis, copies):
    rows, width = basis.shape
    columns = taken.shape[2] // (width // 2 // rows + 1)
    vmem = pl.BlockSpec(memory_space=pltpu.VMEM)
    shapes = [(rows, columns), (copies, columns)]
    return pl.pallas_call(
        residual_kernel,
        out_shape=[jax.ShapeDtypeStruct(shape, jnp.float32) for shape in shapes],
        in_specs=[vmem, vmem],
        out_specs=[vmem] * 2,
        scratch_shapes=[pltpu.VMEM((count, columns), jnp.float32) for count in (rows, width // 2)],
        compiler_params=pltpu.CompilerParams(vmem_limit_bytes=24 * 2**20),
        cost_estimate=pl.CostEstimate(
            flops=12 * rows * width * columns,
            bytes_accessed=4 * (taken.size + basis.size + rows * columns),
            transcendentals=0,
        ),
    )(taken, basis)


def scale_kernel(total_rows, sums, own, taken, coefficients, new_basis):
    unpack(taken, coefficients)
    squares = sums[...] + turn(sums[...], 1.0, 1.0)
    factor = 1.0 / jnp.sqrt(squares / total_rows + 1e-06)
    new_basis[...] = own[...] * factor


def scaled(sums, own, taken, count, total_rows):
    columns = own.shape[1]
    vmem = pl.BlockSpec(memory_space=pltpu.VMEM)
    shapes = [(count, columns), own.shape]
    return pl.pallas_call(
        functools.partial(scale_kernel, total_rows),
        out_shape=[jax.ShapeDtypeStruct(shape, jnp.float32) for shape in shapes],
        in_specs=[vmem] * 3,
        out_specs=[vmem] * 2,
        compiler_params=pltpu.CompilerParams(vmem_limit_bytes=16 * 2**20),
    )(sums, own, taken)


def per_device(impedance, tile_scale, krylov_block, prior_basis):
    columns = krylov_block.shape[1]
    width = prior_basis.shape[1]
    own_rows = prior_basis.shape[0]
    rows = impedance.shape[1]
    ys, row_members, members = (lax.axis_size(axes) for axes in ("y", ROW, PLANE))
    share = rows // members
    lanes = width // 2 // rows * columns
    with jax.named_scope("entries_z"):
        along_z = lax.all_gather(krylov_block, "z", axis=0)
        along_z, prior = lax.optimization_barrier((along_z, prior_basis))
    with jax.named_scope("entries_y"):
        entries = lax.all_to_all(copies_of(along_z, ys), "y", 0, 0, tiled=True)
    with jax.named_scope("basis_rows"):
        here = ring_gather(ring_gather(prior, "core"), "x").reshape(rows, width)
    with jax.named_scope("stage"):
        scales = jnp.repeat(tile_scale, rows // tile_scale.shape[0], axis=0)
        start = (lax.axis_index(ROW) * own_rows).astype(jnp.int32)
        turned = with_layout_constraint(here.T, Layout((0, 1)))
        held = (entries, scales, here, turned, start)
        entries, scales, here, turned, start = lax.optimization_barrier(held)
    with jax.named_scope("slab"):
        parts = slab_sums(impedance, scales, entries, turned, members)
    with jax.named_scope("sums_plane"):
        taken = lax.all_to_all(parts, PLANE, 0, 0, tiled=True)
        chunk = jnp.sum(taken[:, :, :lanes], axis=0)
        product = jnp.sum(taken[:, :, lanes:].reshape(row_members, ys, share, columns), axis=0)
        chunk, product = lax.optimization_barrier((chunk, product))
    with jax.named_scope("coefficients_z"):
        chunk = jnp.sum(spread(chunk, "z"), axis=0)
    with jax.named_scope("gather_plane"):
        parts = jnp.broadcast_to(product[None], (row_members,) + product.shape).reshape(members, share, columns)
        parts = jnp.concatenate([jnp.broadcast_to(chunk[None], (members,) + chunk.shape), parts], 2)
        taken = lax.all_to_all(parts, PLANE, 0, 0, tiled=True)
    with jax.named_scope("residual"):
        residual, sums = rows_residual(taken, here, lax.axis_size(COL))
        zero = jnp.int32(0)
        own = lax.dynamic_slice(residual, (start, zero), (own_rows, columns), allow_negative_indices=False)
        own, sums = lax.optimization_barrier((own, sums))
    with jax.named_scope("squares"):
        sums = jnp.sum(lax.all_to_all(sums, COL, 0, 0, tiled=True), axis=0)
    with jax.named_scope("scale"):
        total_rows = own_rows * lax.axis_size(ROW + COL)
        coefficients, new_basis = scaled(sums[None], own, taken, width // 2, total_rows)
    return (coefficients, new_basis)


def solution(mesh):
    rows = 4 if mesh.shape["row"] % 4 == 0 else 1
    devices = mesh.devices.reshape(rows, mesh.shape["row"] // rows, mesh.shape["col"] // 4, 4)
    fine = Mesh(devices, ("x", "core", "z", "y"))
    return jax.shard_map(
        per_device,
        mesh=fine,
        in_specs=(
            P(None, COL, ROW),
            P(COL, ROW),
            P(ROW + COL, None),
            P(COL + ROW, None),
        ),
        out_specs=(P(), P(COL + ROW, None)),
        check_vma=False,
    )
```

```python
import functools

import jax
import jax.numpy as jnp
from jax import lax
from jax.experimental import pallas as pl
from jax.experimental.pallas import tpu as pltpu
from jax.experimental.layout import Layout, with_layout_constraint
from jax.sharding import Mesh, PartitionSpec as P

ROW = ("x", "core")
COL = ("z", "y")
PLANE = ("x", "core", "y")
HIGHEST = lax.Precision.HIGHEST


def spread(block, axes):
    size = lax.axis_size(axes)
    copies = jnp.broadcast_to(block[None], (size,) + block.shape)
    return lax.all_to_all(copies, axes, 0, 0, tiled=True)


def ring_gather(block, axis):
    size = lax.axis_size(axis)
    me = lax.axis_index(axis)
    stacked = jnp.zeros((size,) + block.shape, block.dtype)
    for step in range(size):
        pairs = [(member, (member + step) % size) for member in range(size)]
        arrived = lax.ppermute(block, axis, pairs) if step else block
        owner = lax.rem(me - step + size, size)
        stacked = lax.dynamic_update_index_in_dim(stacked, arrived, owner, 0)
    return stacked


def turn(block, first, second):
    half = block.shape[1] // 2
    lanes = lax.broadcasted_iota(jnp.int32, block.shape, 1)
    return pltpu.roll(block, half, 1) * jnp.where(lanes < half, first, second)


def copies_kernel(source, out, sems):
    size = out.shape[0]
    copies = [pltpu.make_async_copy(source, out.at[i], sems.at[i]) for i in range(size)]
    for copy in copies:
        copy.start()
    for copy in copies:
        copy.wait()


def copies_of(block, size):
    return pl.pallas_call(
        copies_kernel,
        out_shape=jax.ShapeDtypeStruct((size,) + block.shape, block.dtype),
        in_specs=[pl.BlockSpec(memory_space=pltpu.VMEM)],
        out_specs=pl.BlockSpec(memory_space=pltpu.HBM),
        scratch_shapes=[pltpu.SemaphoreType.DMA((size,))],
        compiler_params=pltpu.CompilerParams(vmem_limit_bytes=8 * 2**20),
    )(block)


def slab_kernel(chunks, impedance, scales, entries, basis, out, held, sems):
    rows, columns = scales.shape[0], entries.shape[3]
    ys, zs, depth, _ = entries.shape
    width = ys * depth
    members, share, _ = out.shape
    span = zs * width // chunks
    copies = []
    for chunk in range(chunks):
        part = pl.ds(chunk * span, span)
        copies.append(pltpu.make_async_copy(impedance.at[:, :, part], held.at[:, :, part], sems.at[chunk]))
        copies[-1].start()
    running = jnp.zeros((2, rows, columns), jnp.float32)
    for tile in range(zs):
        if tile % (zs // chunks) == 0:
            copies[tile // (zs // chunks)].wait()
        piece = held[:, :, tile * width : (tile + 1) * width].reshape(2 * rows, width)
        block = entries[:, tile].reshape(width, columns)
        product = jnp.dot(piece, block, preferred_element_type=jnp.float32)
        running += product.reshape(2, rows, columns) * scales[:, tile : tile + 1][None]
    partial = running[0] + turn(running[1], -1.0, 1.0)
    inner = jnp.dot(basis[...], partial, precision=HIGHEST, preferred_element_type=jnp.float32)
    half = columns // 2
    inner = inner.reshape(-1, 2, half, columns)
    sums = inner[:, 0].reshape(-1, columns) + turn(inner[:, 1].reshape(-1, columns), 1.0, -1.0)
    step = sums.shape[0] // members
    for member in range(members):
        for first in range(0, step, share):
            lanes = slice(first // share * columns, (first // share + 1) * columns)
            out[member, :, lanes] = sums[member * step + first : member * step + first + share]
        out[member, :, step // share * columns :] = partial[member * share : (member + 1) * share]


def slab_sums(impedance, scales, entries, basis, members):
    rows = impedance.shape[1]
    columns = entries.shape[3]
    chunks = 2
    share = rows // members
    lanes = (basis.shape[0] // 2 // rows + 1) * columns
    vmem = pl.BlockSpec(memory_space=pltpu.VMEM)
    return pl.pallas_call(
        functools.partial(slab_kernel, chunks),
        out_shape=jax.ShapeDtypeStruct((members, share, lanes), jnp.float32),
        in_specs=[pl.BlockSpec(memory_space=pltpu.HBM), vmem, vmem, vmem],
        out_specs=vmem,
        scratch_shapes=[pltpu.VMEM(impedance.shape, impedance.dtype), pltpu.SemaphoreType.DMA((chunks,))],
        compiler_params=pltpu.CompilerParams(vmem_limit_bytes=48 * 2**20),
        cost_estimate=pl.CostEstimate(
            flops=4 * impedance.shape[2] * rows * columns,
            bytes_accessed=2 * (impedance.size + entries.size),
            transcendentals=0,
        ),
    )(impedance, scales, entries, basis)


def unpack(taken, found):
    members, share, _ = taken.shape
    columns = found.shape[1]
    step = found.shape[0] // members
    for member in range(members):
        for first in range(0, step, share):
            lanes = slice(first // share * columns, (first // share + 1) * columns)
            found[member * step + first : member * step + first + share] = taken[member, :, lanes]


def residual_kernel(taken, basis, residual, sums, product, found):
    members, share, _ = taken.shape
    rows, width = basis.shape
    count, columns = found.shape
    half = columns // 2
    for member in range(members):
        product[member * share : (member + 1) * share] = taken[member, :, count // rows * columns :]
    unpack(taken, found)
    turned = turn(found[...], -1.0, 1.0)
    pair = [found[...].reshape(-1, 1, half, columns), turned.reshape(-1, 1, half, columns)]
    both = jnp.concatenate(pair, 1).reshape(width, columns)
    known = jnp.dot(basis[...], both, precision=HIGHEST, preferred_element_type=jnp.float32)
    rest = product[...] - known
    residual[...] = rest
    sums[...] = jnp.broadcast_to(jnp.sum(rest * rest, axis=0, keepdims=True), sums.shape)


def rows_residual(taken, basis, copies):
    rows, width = basis.shape
    columns = taken.shape[2] // (width // 2 // rows + 1)
    vmem = pl.BlockSpec(memory_space=pltpu.VMEM)
    shapes = [(rows, columns), (copies, columns)]
    return pl.pallas_call(
        residual_kernel,
        out_shape=[jax.ShapeDtypeStruct(shape, jnp.float32) for shape in shapes],
        in_specs=[vmem, vmem],
        out_specs=[vmem] * 2,
        scratch_shapes=[pltpu.VMEM((count, columns), jnp.float32) for count in (rows, width // 2)],
        compiler_params=pltpu.CompilerParams(vmem_limit_bytes=24 * 2**20),
        cost_estimate=pl.CostEstimate(
            flops=12 * rows * width * columns,
            bytes_accessed=4 * (taken.size + basis.size + rows * columns),
            transcendentals=0,
        ),
    )(taken, basis)


def scale_kernel(total_rows, sums, own, taken, coefficients, new_basis):
    unpack(taken, coefficients)
    squares = sums[...] + turn(sums[...], 1.0, 1.0)
    factor = 1.0 / jnp.sqrt(squares / total_rows + 1e-06)
    new_basis[...] = own[...] * factor


def scaled(sums, own, taken, count, total_rows):
    columns = own.shape[1]
    vmem = pl.BlockSpec(memory_space=pltpu.VMEM)
    shapes = [(count, columns), own.shape]
    return pl.pallas_call(
        functools.partial(scale_kernel, total_rows),
        out_shape=[jax.ShapeDtypeStruct(shape, jnp.float32) for shape in shapes],
        in_specs=[vmem] * 3,
        out_specs=[vmem] * 2,
        compiler_params=pltpu.CompilerParams(vmem_limit_bytes=16 * 2**20),
    )(sums, own, taken)


def per_device(impedance, tile_scale, krylov_block, prior_basis):
    columns = krylov_block.shape[1]
    width = prior_basis.shape[1]
    own_rows = prior_basis.shape[0]
    rows = impedance.shape[1]
    ys, row_members, members = (lax.axis_size(axes) for axes in ("y", ROW, PLANE))
    share = rows // members
    lanes = width // 2 // rows * columns
    with jax.named_scope("entries_z"):
        along_z = lax.all_gather(krylov_block, "z", axis=0)
        along_z, prior = lax.optimization_barrier((along_z, prior_basis))
    with jax.named_scope("entries_y"):
        entries = lax.all_to_all(copies_of(along_z, ys), "y", 0, 0, tiled=True)
    with jax.named_scope("basis_rows"):
        here = ring_gather(ring_gather(prior, "core"), "x").reshape(rows, width)
    with jax.named_scope("stage"):
        scales = jnp.repeat(tile_scale, rows // tile_scale.shape[0], axis=0)
        start = (lax.axis_index(ROW) * own_rows).astype(jnp.int32)
        turned = with_layout_constraint(here.T, Layout((0, 1)))
        held = (entries, scales, here, turned, start)
        entries, scales, here, turned, start = lax.optimization_barrier(held)
    with jax.named_scope("slab"):
        parts = slab_sums(impedance, scales, entries, turned, members)
    with jax.named_scope("sums_plane"):
        taken = lax.all_to_all(parts, PLANE, 0, 0, tiled=True)
        chunk = jnp.sum(taken[:, :, :lanes], axis=0)
        product = jnp.sum(taken[:, :, lanes:].reshape(row_members, ys, share, columns), axis=0)
        chunk, product = lax.optimization_barrier((chunk, product))
    with jax.named_scope("coefficients_z"):
        chunk = jnp.sum(spread(chunk, "z"), axis=0)
    with jax.named_scope("gather_plane"):
        parts = jnp.broadcast_to(product[None], (row_members,) + product.shape).reshape(members, share, columns)
        parts = jnp.concatenate([jnp.broadcast_to(chunk[None], (members,) + chunk.shape), parts], 2)
        taken = lax.all_to_all(parts, PLANE, 0, 0, tiled=True)
    with jax.named_scope("residual"):
        residual, sums = rows_residual(taken, here, lax.axis_size(COL))
        zero = jnp.int32(0)
        own = lax.dynamic_slice(residual, (start, zero), (own_rows, columns), allow_negative_indices=False)
        own, sums = lax.optimization_barrier((own, sums))
    with jax.named_scope("squares"):
        sums = jnp.sum(lax.all_to_all(sums, COL, 0, 0, tiled=True), axis=0)
    with jax.named_scope("scale"):
        total_rows = own_rows * lax.axis_size(ROW + COL)
        coefficients, new_basis = scaled(sums[None], own, taken, width // 2, total_rows)
    return (coefficients, new_basis)


def solution(mesh):
    rows = 4 if mesh.shape["row"] % 4 == 0 else 1
    devices = mesh.devices.reshape(rows, mesh.shape["row"] // rows, mesh.shape["col"] // 4, 4)
    fine = Mesh(devices, ("x", "core", "z", "y"))
    return jax.shard_map(
        per_device,
        mesh=fine,
        in_specs=(
            P(None, COL, ROW),
            P(COL, ROW),
            P(ROW + COL, None),
            P(COL + ROW, None),
        ),
        out_specs=(P(), P(COL + ROW, None)),
        check_vma=False,
    )
```
